32 devices in a mesh: freq: 8 (over y, x, core), row: 4 (over z).
Axes of the slice: x: 2, y: 2, z: 4, core: 2. Of those that a mesh axis runs over, the one named last changes fastest.
Arguments:
- source: bfloat16 [8, 2, 64, 512], P('freq', None, 'row'), may hold values from -6 to 6
- receiver: bfloat16 [8, 2, 64, 512], P('freq', None, 'row'), may hold values from -6 to 6
- filters: bfloat16 [8, 2, 2, 25, 25], P('freq'), may hold values from -0.15625 to 0.15625
- table_index: int32 [2, 64, 512], P(None, 'row'), may hold values from 0 to 1
- lags: int32 [16], replicated, may hold values from 0 to 15, each once
- offset_filters: float32 [16, 9, 9], P('freq'), may hold values from -0.15625 to 0.15625
Outputs:
- image: float32 [2, 16, 64, 512], P(None, 'freq', 'row')
The draws below stay inside these ranges and needn't reach their ends.
Inputs may be any that keep to these rules, and one draw needn't show every extreme that they name: `lags`: each of 0 .. 15 appears exactly once.
All inputs are finite; a program needn't handle non-finite values.
Results may differ from the reference program's by a relative error of at most 0.0052.
Values may be sent and summed in bfloat16 or wider, within the bound.
A program may use at most 128 MiB of HBM per device.

```python
import jax
import jax.numpy as jnp
from jax import lax

NY = 512
NV = 2
FILT = 25
NOFF = 16
OFILT = 9
DEPTHS = 2
FREQS = 8
NX = 64


def set_ends(entries, stream_key, least, largest):
    spot = [jax.random.randint(jax.random.fold_in(stream_key, axis), (), 0, length) for axis, length in enumerate(entries.shape)]
    main_axis = entries.shape.index(max(entries.shape))
    neighbour = spot[:main_axis] + [(spot[main_axis] + 1) % entries.shape[main_axis]] + spot[main_axis + 1:]
    return entries.at[tuple(spot)].set(least).at[tuple(neighbour)].set(largest)


def levels(key, dims, cuts, smallest, top_value):
    loudness = 1.0
    for dim, parts in cuts:
        heights = jax.random.uniform(jax.random.fold_in(jax.random.fold_in(key, 6), dim), (parts,), jnp.float32, smallest / len(cuts), top_value / len(cuts))
        loudness = loudness * jnp.repeat(jnp.exp(heights), dims[dim] // parts).reshape((-1,) + (1,) * (len(dims) - 1 - dim))
    return loudness


def bell_draw(stream_key, shape, deviation, reach, pieces=(), kind=jnp.bfloat16):
    values = deviation * jax.random.normal(stream_key, shape, jnp.float32)
    if pieces:
        values = values * levels(stream_key, shape, pieces, -0.22, 0.18)
    return jnp.clip(values, -reach, reach).astype(kind)


def setup_inputs(seed: int = 0) -> dict:
    splits = jax.random.split(jax.random.key(seed), 7)
    source = bell_draw(splits[0], (FREQS, 2, NX, NY), 1.0, 6.0, ((0, 8), (2, 4)))
    receiver = bell_draw(splits[1], (FREQS, 2, NX, NY), 1.0, 6.0, ((0, 8), (2, 4)))
    filters = bell_draw(splits[2], (FREQS, NV, 2, FILT, FILT), (2 * FILT * FILT) ** -0.5, 0.15625, ((0, 8),))
    table_index = set_ends(jax.random.randint(splits[3], (DEPTHS, NX, NY), 0, NV), jax.random.fold_in(splits[3], 1), 0, NV - 1).astype(jnp.int32)
    lags = jax.random.permutation(splits[4], NOFF).astype(jnp.int32)
    offset_filters = bell_draw(splits[5], (NOFF, OFILT, OFILT), (2 * OFILT * OFILT * FREQS) ** -0.5, 0.15625, ((0, 8),), jnp.float32)
    return dict(source=source, receiver=receiver, filters=filters, table_index=table_index, lags=lags, offset_filters=offset_filters)


def kernel_of(taps, sign):
    real_part = taps[:, 0].astype(jnp.float32)
    imag_part = taps[:, 1].astype(jnp.float32) * sign
    upper = jnp.stack([real_part, -imag_part], 1)
    lower = jnp.stack([imag_part, real_part], 1)
    kernel = jnp.stack([upper, lower], 1)
    return kernel.reshape((NV * 2, 2, FILT, FILT))


def extrapolate(field, filters, index, sign):
    half = (FILT - 1) // 2
    classes = jnp.arange(NV, dtype=jnp.int32)
    hot = (index[None, :, :] == classes[:, None, None]).astype(jnp.float32)

    def one_freq(pair):
        plane, taps = pair
        out = lax.conv_general_dilated(plane[None].astype(jnp.float32), kernel_of(taps, sign), (1, 1),
                                       ((half, half), (half, half)),
                                       dimension_numbers=("NCHW", "OIHW", "NCHW"),
                                       precision=lax.Precision.HIGHEST)[0]
        out = out.reshape((NV, 2, NX, NY))
        return jnp.sum(out * hot[:, None], axis=0).astype(jnp.bfloat16)

    return lax.map(one_freq, (field, filters))


def correlate(source, receiver, lags):
    shift = NOFF // 2
    down_pad = jnp.pad(source, ((0, 0), (0, 0), (0, 0), (shift, shift)))
    up_pad = jnp.pad(receiver, ((0, 0), (0, 0), (0, 0), (shift, shift)))

    def one_lag(lag):
        offset = lag.astype(jnp.int32) - shift
        down = lax.dynamic_slice_in_dim(down_pad, (shift - offset).astype(jnp.int32), NY, 3)
        up = lax.dynamic_slice_in_dim(up_pad, (shift + offset).astype(jnp.int32), NY, 3)
        return jnp.sum(down.astype(jnp.float32) * up.astype(jnp.float32), axis=(0, 1))

    return lax.map(one_lag, lags)


def reference(source, receiver, filters, table_index, lags, offset_filters):
    ohalf = (OFILT - 1) // 2
    raws = []
    for depth in range(DEPTHS):
        source = extrapolate(source, filters, table_index[depth], 1.0)
        receiver = extrapolate(receiver, filters, table_index[depth], -1.0)
        raws.append(correlate(source, receiver, lags))
    raw = jnp.stack(raws)
    kernel = offset_filters[:, None].astype(jnp.float32)
    return lax.conv_general_dilated(raw, kernel, (1, 1), ((ohalf, ohalf), (ohalf, ohalf)),
                                    dimension_numbers=("NCHW", "OIHW", "NCHW"),
                                    feature_group_count=NOFF,
                                    precision=lax.Precision.HIGHEST)
```

```python
import functools

import jax
import jax.numpy as jnp
from jax import lax
from jax.experimental import pallas as pl
from jax.experimental.pallas import tpu as pltpu
from jax.sharding import PartitionSpec as P

MESH = pl.DeviceIdType.MESH
GROUP = 5
LANES = 128


def filter_matrix(taps, filt, rows):
    nv = taps.shape[0] // 2
    window = 3 * rows
    lead = rows - (filt - 1) // 2
    groups = -(-filt // GROUP)
    depth = -(-(GROUP * 2 * window) // LANES) * LANES
    at = lax.broadcasted_iota(jnp.int32, (taps.shape[2], depth), 1)
    first = lax.broadcasted_iota(jnp.int32, (taps.shape[2], depth), 0)
    section = lax.div(at, window)
    place = (at - section * window == first + lead) & (section < 2 * GROUP)
    place = place.astype(jnp.float32).astype(jnp.bfloat16)
    columns = taps.shape[1]
    first, section = first[:columns], section[:columns]
    kept = lax.rem(first, GROUP) == lax.div(section, 2)
    real_in = lax.rem(section, 2) == 0
    group_of = lax.div(lax.broadcasted_iota(jnp.int32, (groups * rows, columns), 0), rows)
    spread = lax.div(lax.broadcasted_iota(jnp.int32, (groups * rows, columns), 1), GROUP) == group_of
    spread = spread.astype(jnp.float32).astype(jnp.bfloat16)
    blocks = []
    for v in range(nv):
        real, imag = (
            jnp.where(kept, jnp.dot(taps[2 * v + i], place, preferred_element_type=jnp.float32), 0.0)
            for i in range(2)
        )
        for out in (jnp.where(real_in, real, -imag), jnp.where(real_in, imag, real)):
            blocks.append(jnp.dot(spread, out.astype(jnp.bfloat16), preferred_element_type=jnp.float32))
    tall = jnp.concatenate(
        [block[g * rows : (g + 1) * rows] for g in range(groups) for block in blocks], axis=0
    )
    row_ids = lax.rem(lax.broadcasted_iota(jnp.int32, tall.shape, 0), rows)
    move = 1
    while move < rows:
        tall = jnp.where(row_ids & move != 0, pltpu.roll(tall, move, 1), tall)
        move *= 2
    return tall.astype(jnp.bfloat16)


def kernel(
    nf,
    nr,
    filt,
    source,
    receiver,
    taps,
    index,
    lags,
    ofilters,
    image,
    matrix,
    shifted,
    field,
    halo,
    fsend,
    fgot,
    by_lag,
    rsend,
    rgot,
    plane,
    hs_sem,
    hr_sem,
    fs_sem,
    fr_sem,
    rs_sem,
    rr_sem,
    es_sem,
):
    depths, rows, width = index.shape
    noff = lags.shape[0]
    ofilt, kper, _ = ofilters.shape
    ohalf = (ofilt - 1) // 2
    per = rows // nf
    edge = ohalf // per
    wide = width + LANES
    groups = -(-filt // GROUP)
    nv = matrix.shape[0] // (groups * 2 * rows)

    f = lax.axis_index("freq")
    r = lax.axis_index("row")
    before, after = lax.rem(r + nr - 1, nr), lax.rem(r + 1, nr)
    has_left = r > 0
    has_right = r < nr - 1
    low = f < edge
    high = f >= nf - edge

    barrier = pltpu.get_barrier_semaphore()

    def greet(ff, rr):
        pl.semaphore_signal(barrier, inc=1, device_id=(ff, rr), device_id_type=MESH)

    @pl.when(has_left)
    def _():
        for p in range(nf - edge, nf):
            greet(p, before)

        @pl.when(f < nf - edge)
        def _():
            greet(f, before)

    @pl.when(has_right)
    def _():
        for p in range(edge):
            greet(p, after)

        @pl.when(f >= edge)
        def _():
            greet(f, after)

    for j in range(1, nf):
        greet(lax.rem(f + j, nf), r)

    def clear(side, first):
        for depth in range(depths):
            for g in range(2):
                for c in range(2):
                    halo[depth, side, g, c] = jnp.zeros((rows, width), halo.dtype)
            for p in range(edge):
                rgot[depth, first + p] = jnp.zeros(rgot.shape[2:], rgot.dtype)

    @pl.when(r < 1)
    def _():
        clear(0, 0)

    @pl.when(r >= nr - 1)
    def _():
        clear(1, edge + nf)

    pl.semaphore_wait(
        barrier,
        nf
        - 1
        + jnp.where(has_left, jnp.where(low, nf, 1), 0)
        + jnp.where(has_right, jnp.where(high, nf, 1), 0),
    )

    def halo_copy(depth, g, side, to):
        src = (source, receiver)[g].at[0] if depth == 0 else field.at[g]
        return pltpu.make_async_remote_copy(
            src_ref=src,
            dst_ref=halo.at[depth, side, g],
            send_sem=hs_sem.at[(depth * 2 + side) * 2 + g],
            recv_sem=hr_sem.at[(depth * 2 + side) * 2 + g],
            device_id=(f, to),
            device_id_type=MESH,
        )

    def halo_start(depth):
        @pl.when(has_right)
        def _():
            for g in range(2):
                halo_copy(depth, g, 0, after).start()

        @pl.when(has_left)
        def _():
            for g in range(2):
                halo_copy(depth, g, 1, before).start()

    def halo_recv(depth):
        @pl.when(has_left)
        def _():
            for g in range(2):
                halo_copy(depth, g, 0, before).wait_recv()

        @pl.when(has_right)
        def _():
            for g in range(2):
                halo_copy(depth, g, 1, after).wait_recv()

    def halo_sent(depth):
        @pl.when(has_right)
        def _():
            for g in range(2):
                halo_copy(depth, g, 0, after).wait_send()

        @pl.when(has_left)
        def _():
            for g in range(2):
                halo_copy(depth, g, 1, before).wait_send()

    def field_copy(depth, j):
        return pltpu.make_async_remote_copy(
            src_ref=fsend.at[depth, lax.rem(f + j, nf)],
            dst_ref=fgot.at[depth, j - 1],
            send_sem=fs_sem.at[depth * (nf - 1) + j - 1],
            recv_sem=fr_sem.at[depth * (nf - 1) + j - 1],
            device_id=(lax.rem(f + j, nf), r),
            device_id_type=MESH,
        )

    def raw_copy(depth, p, to, slot, sem):
        return pltpu.make_async_remote_copy(
            src_ref=rsend.at[depth, p],
            dst_ref=rgot.at[depth, slot],
            send_sem=sem,
            recv_sem=rr_sem.at[depth * (nf + 2 * edge) + slot],
            device_id=(p, to),
            device_id_type=MESH,
        )

    def raw_sends(depth, act):
        for j in range(1, nf):
            p = lax.rem(f + j, nf)
            act(raw_copy(depth, p, r, edge + f, rs_sem.at[depth * (nf - 1) + j - 1]))

        @pl.when(has_left)
        def _():
            @pl.when(low)
            def _():
                for p in range(nf):
                    act(raw_copy(depth, p, before, edge + nf + lax.rem(f, edge), es_sem.at[(depth * 2) * nf + p]))

        @pl.when(has_right)
        def _():
            @pl.when(high)
            def _():
                for p in range(nf):
                    slot = lax.rem(f + edge * nf - nf, edge)
                    act(raw_copy(depth, p, after, slot, es_sem.at[(depth * 2 + 1) * nf + p]))

    def raw_recv(depth):
        def wait(slot):
            raw_copy(depth, lax.rem(f + 1, nf), r, slot, rs_sem.at[depth * (nf - 1)]).wait_recv()

        for j in range(1, nf):
            wait(edge + lax.rem(f + j, nf))

        @pl.when(has_left)
        def _():
            for p in range(edge):
                wait(p)

        @pl.when(has_right)
        def _():
            for p in range(edge):
                wait(edge + nf + p)

    def filled(parts):
        count = sum(part.shape[0] for part in parts)
        if count % 8:
            parts = parts + [jnp.zeros((-count % 8, parts[0].shape[1]), parts[0].dtype)]
        return jnp.concatenate(parts, axis=0)

    def widen(value):
        zeros = jnp.zeros((value.shape[0], wide - width), value.dtype)
        return jnp.concatenate([value, zeros], axis=1)

    def step(depth):
        taken = jnp.concatenate([index[depth]] * 2, axis=0)
        window = 6 * rows
        for g in range(2):
            parts = []
            for c in range(2):
                part = c if g == 0 else 1 - c
                own = (source, receiver)[g][0, part] if depth == 0 else field[g, part]
                parts += [halo[depth, 0, g, part], own, halo[depth, 1, g, part]]
            tall = widen(jnp.concatenate(parts, axis=0).astype(jnp.float32))
            for b in range(GROUP):
                turn = (GROUP // 2 - b) % wide
                moved = pltpu.roll(tall, turn, 1) if turn else tall
                shifted[g, b * window : (b + 1) * window, :] = moved.astype(jnp.bfloat16)
        chosen = []
        for g in range(2):
            product = jnp.dot(matrix[...], shifted[g], preferred_element_type=jnp.float32)
            block = nv * 2 * rows
            total = None
            for b in range(groups):
                term = product[b * block : (b + 1) * block]
                turn = (-GROUP * (b - groups // 2)) % wide
                term = pltpu.roll(term, turn, 1) if turn else term
                total = term if total is None else total + term
            total = total[:, :width]
            out = total[: 2 * rows]
            for v in range(1, nv):
                out = jnp.where(taken == v, total[v * 2 * rows : (v + 1) * 2 * rows], out)
            chosen.append(out)
        return chosen

    def scatter_fields(depth, chosen):
        sections = [chosen[0][:rows], chosen[0][rows:], chosen[1][rows:], chosen[1][:rows]]
        for p in range(nf):
            piece = [s[p * per : (p + 1) * per] for s in sections]
            piece = filled(piece)
            piece = jnp.concatenate([piece[:, : width // 2], piece[:, width // 2 :]], axis=0)
            fsend[depth, p] = piece.astype(jnp.bfloat16)
        for j in range(1, nf):
            field_copy(depth, j).start()

    def correlate(depth):
        for j in range(1, nf):
            field_copy(depth, j).wait_recv()
        downs, ups = [], []
        for j in range(nf):
            piece = fsend[depth, f] if j == 0 else fgot[depth, j - 1]
            piece = piece.astype(jnp.float32)
            tile = piece.shape[0] // 2
            piece = jnp.concatenate([piece[:tile], piece[tile:]], axis=1)
            downs.append(piece[: 2 * per])
            ups.append(piece[2 * per : 4 * per])
        down = widen(jnp.concatenate(downs, axis=0))
        up = widen(jnp.concatenate(ups, axis=0))
        shift = noff // 2
        for lag in range(noff):
            offset = lag - shift
            turn = (-2 * offset) % wide
            terms = down * (pltpu.roll(up, turn, 1) if turn else up)
            total = terms[:8]
            for i in range(1, terms.shape[0] // 8):
                total = total + terms[8 * i : 8 * i + 8]
            turn = offset % wide
            total = (pltpu.roll(total, turn, 1) if turn else total)[:, :width]
            raw = total[:per]
            for i in range(1, 8 // per):
                raw = raw + total[i * per : (i + 1) * per]
            by_lag[lag] = filled([raw[:, : width // 2], raw[:, width // 2 :]])
        for p in range(nf):
            rsend[depth, p] = filled([by_lag[lags[p * kper + k]][: 2 * per] for k in range(kper)])
        raw_sends(depth, lambda copy: copy.start())
        rgot[depth, edge + f] = rsend[depth, f]

    def filter_images(depth):
        raw_recv(depth)
        pieces = [rgot[depth, s] for s in range(nf + 2 * edge)]
        for k in range(kper):
            left, right = (
                jnp.concatenate([piece[at : at + per] for piece in pieces], axis=0)
                for at in (2 * per * k, 2 * per * k + per)
            )
            plane[k] = widen(jnp.concatenate([left, right], axis=1))
        for k in range(kper):
            total = None
            for b in range(ofilt):
                column = None
                for a in range(ofilt):
                    term = ofilters[a, k, b] * plane[k, a : a + rows, :]
                    column = term if column is None else column + term
                turn = (ohalf - b) % wide
                column = (pltpu.roll(column, turn, 1) if turn else column)[:, :width]
                total = column if total is None else total + column
            image[depth, k] = total

    halo_start(0)

    matrix[...] = filter_matrix(taps, filt, rows)
    spare = shifted.shape[1] - GROUP * 6 * rows
    if spare:
        for g in range(2):
            shifted[g, GROUP * 6 * rows :, :] = jnp.zeros((spare, wide), jnp.bfloat16)

    halo_recv(0)
    for depth in range(depths):
        chosen = step(depth)
        if depth + 1 < depths:
            if depth:
                halo_sent(depth)
            for g in range(2):
                field[g, 0] = chosen[g][g * rows : (g + 1) * rows].astype(jnp.bfloat16)
                field[g, 1] = chosen[g][(1 - g) * rows : (2 - g) * rows].astype(jnp.bfloat16)
            halo_start(depth + 1)
        scatter_fields(depth, chosen)
        if depth + 1 < depths:
            halo_recv(depth + 1)
    for depth in range(depths):
        correlate(depth)
    for depth in range(depths):
        filter_images(depth)
    for depth in range(depths):
        if depth == 0 or depth + 1 == depths:
            halo_sent(depth)
        for j in range(1, nf):
            field_copy(depth, j).wait_send()
        raw_sends(depth, lambda copy: copy.wait_send())


def body(nf, nr, source, receiver, filters, table_index, lags, offset_filters):
    depths, rows, width = table_index.shape
    noff = lags.shape[0]
    kper, ofilt, _ = offset_filters.shape
    per = rows // nf
    edge = (ofilt - 1) // 2 // per
    wide = width + LANES
    nv, filt = filters.shape[1], filters.shape[3]
    taps = filters.transpose(0, 1, 2, 4, 3).reshape(nv * 2, filt, filt)
    taps = jnp.pad(taps, ((0, 0), (0, -filt % 32), (0, -filt % LANES)))
    groups = -(-filt // GROUP)
    contracted = -(-(GROUP * 6 * rows) // LANES) * LANES
    piece = -(-4 * per // 8) * 16
    image_piece = -(-2 * per * kper // 8) * 8
    half = width // 2
    vmem = pl.BlockSpec(memory_space=pltpu.VMEM)
    smem = pl.BlockSpec(memory_space=pltpu.SMEM)
    dma = pltpu.SemaphoreType.DMA
    return pl.pallas_call(
        functools.partial(kernel, nf, nr, filt),
        out_shape=jax.ShapeDtypeStruct((depths, kper, rows, width), jnp.float32),
        in_specs=[vmem, vmem, vmem, vmem, smem, smem],
        out_specs=vmem,
        scratch_shapes=[
            pltpu.VMEM((groups * nv * 2 * rows, contracted), jnp.bfloat16),
            pltpu.VMEM((2, contracted, wide), jnp.bfloat16),
            pltpu.VMEM((2, 2, rows, width), jnp.bfloat16),
            pltpu.VMEM((depths, 2, 2, 2, rows, width), jnp.bfloat16),
            pltpu.VMEM((depths, nf, piece, half), jnp.bfloat16),
            pltpu.VMEM((depths, nf - 1, piece, half), jnp.bfloat16),
            pltpu.VMEM((noff, -(-2 * per // 8) * 8, half), jnp.float32),
            pltpu.VMEM((depths, nf, image_piece, half), jnp.float32),
            pltpu.VMEM((depths, nf + 2 * edge, image_piece, half), jnp.float32),
            pltpu.VMEM((kper, rows + ofilt - 1, wide), jnp.float32),
            dma((depths * 4,)),
            dma((depths * 4,)),
            dma((depths * (nf - 1),)),
            dma((depths * (nf - 1),)),
            dma((depths * (nf - 1),)),
            dma((depths * (nf + 2 * edge),)),
            dma((depths * 2 * nf,)),
        ],
        compiler_params=pltpu.CompilerParams(
            collective_id=0, has_side_effects=True, vmem_limit_bytes=48 * 1024 * 1024
        ),
    )(source, receiver, taps, table_index, lags, offset_filters.transpose(1, 0, 2))


def solution(mesh):
    in_specs = (
        P("freq", None, "row", None),
        P("freq", None, "row", None),
        P("freq", None, None, None, None),
        P(None, "row", None),
        P(),
        P("freq", None, None),
    )
    out_specs = P(None, "freq", "row", None)
    return jax.shard_map(
        functools.partial(body, mesh.shape["freq"], mesh.shape["row"]),
        mesh=mesh,
        in_specs=in_specs,
        out_specs=out_specs,
        check_vma=False,
    )
```

```python
import functools

import jax
import jax.numpy as jnp
from jax import lax
from jax.experimental import pallas as pl
from jax.experimental.pallas import tpu as pltpu
from jax.sharding import PartitionSpec as P

MESH = pl.DeviceIdType.MESH
GROUP = 5
LANES = 128
ROLLED = jnp.bfloat16


def filter_matrix(taps, filt, rows):
    nv = taps.shape[0] // 2
    window = 3 * rows
    lead = rows - (filt - 1) // 2
    groups = -(-filt // GROUP)
    depth = -(-(GROUP * 2 * window) // LANES) * LANES
    at = lax.broadcasted_iota(jnp.int32, (taps.shape[2], depth), 1)
    first = lax.broadcasted_iota(jnp.int32, (taps.shape[2], depth), 0)
    section = lax.div(at, window)
    place = (at - section * window == first + lead) & (section < 2 * GROUP)
    place = place.astype(jnp.float32).astype(jnp.bfloat16)
    columns = taps.shape[1]
    first, section = first[:columns], section[:columns]
    kept = lax.rem(first, GROUP) == lax.div(section, 2)
    real_in = lax.rem(section, 2) == 0
    group_of = lax.div(lax.broadcasted_iota(jnp.int32, (groups * rows, columns), 0), rows)
    spread = lax.div(lax.broadcasted_iota(jnp.int32, (groups * rows, columns), 1), GROUP) == group_of
    spread = spread.astype(jnp.float32).astype(jnp.bfloat16)
    blocks = []
    for v in range(nv):
        real, imag = (
            jnp.where(kept, jnp.dot(taps[2 * v + i], place, preferred_element_type=jnp.float32), 0.0)
            for i in range(2)
        )
        for out in (jnp.where(real_in, real, -imag), jnp.where(real_in, imag, real)):
            blocks.append(jnp.dot(spread, out.astype(jnp.bfloat16), preferred_element_type=jnp.float32))
    tall = jnp.concatenate(
        [block[g * rows : (g + 1) * rows] for g in range(groups) for block in blocks], axis=0
    )
    row_ids = lax.rem(lax.broadcasted_iota(jnp.int32, tall.shape, 0), rows)
    move = 1
    while move < rows:
        tall = jnp.where(row_ids & move != 0, pltpu.roll(tall, move, 1), tall)
        move *= 2
    return tall.astype(jnp.bfloat16)


def kernel(
    nf,
    nr,
    filt,
    source,
    receiver,
    taps,
    index,
    lags,
    ofilters,
    image,
    table,
    matrix,
    shifted,
    field,
    halo,
    fsend,
    fgot,
    by_lag,
    rsend,
    rgot,
    plane,
    hs_sem,
    hr_sem,
    fs_sem,
    fr_sem,
    rs_sem,
    rr_sem,
    es_sem,
    in_sem,
):
    depths, rows, width = index.shape
    noff = lags.shape[0]
    ofilt, kper, _ = ofilters.shape
    ohalf = (ofilt - 1) // 2
    per = rows // nf
    edge = ohalf // per
    wide = width + LANES
    groups = -(-filt // GROUP)
    nv = matrix.shape[0] // (groups * 2 * rows)

    f = lax.axis_index("freq")
    r = lax.axis_index("row")
    before, after = lax.rem(r + nr - 1, nr), lax.rem(r + 1, nr)
    has_left = r > 0
    has_right = r < nr - 1
    low = f < edge
    high = f >= nf - edge

    loads = [
        pltpu.make_async_copy(source.at[0], field.at[0, 0], in_sem.at[0]),
        pltpu.make_async_copy(receiver.at[0], field.at[0, 1], in_sem.at[1]),
        pltpu.make_async_copy(index, table, in_sem.at[2]),
    ]
    for load in loads:
        load.start()

    barrier = pltpu.get_barrier_semaphore()

    def greet(ff, rr):
        pl.semaphore_signal(barrier, inc=1, device_id=(ff, rr), device_id_type=MESH)

    @pl.when(has_left)
    def _():
        for p in range(nf - edge, nf):
            greet(p, before)

        @pl.when(f < nf - edge)
        def _():
            greet(f, before)

    @pl.when(has_right)
    def _():
        for p in range(edge):
            greet(p, after)

        @pl.when(f >= edge)
        def _():
            greet(f, after)

    for j in range(1, nf):
        greet(lax.rem(f + j, nf), r)

    def clear(side, first):
        for depth in range(depths):
            for g in range(2):
                for c in range(2):
                    halo[depth, side, g, c] = jnp.zeros((rows, width), halo.dtype)
            for p in range(edge):
                rgot[depth, first + p] = jnp.zeros(rgot.shape[2:], rgot.dtype)

    @pl.when(r < 1)
    def _():
        clear(0, 0)

    @pl.when(r >= nr - 1)
    def _():
        clear(1, edge + nf)

    pl.semaphore_wait(
        barrier,
        nf
        - 1
        + jnp.where(has_left, jnp.where(low, nf, 1), 0)
        + jnp.where(has_right, jnp.where(high, nf, 1), 0),
    )

    def halo_copy(depth, g, side, to):
        src = (source, receiver)[g].at[0] if depth == 0 else field.at[depth, g]
        return pltpu.make_async_remote_copy(
            src_ref=src,
            dst_ref=halo.at[depth, side, g],
            send_sem=hs_sem.at[(depth * 2 + side) * 2 + g],
            recv_sem=hr_sem.at[(depth * 2 + side) * 2 + g],
            device_id=(f, to),
            device_id_type=MESH,
        )

    def halo_start(depth, g):
        @pl.when(has_right)
        def _():
            halo_copy(depth, g, 0, after).start()

        @pl.when(has_left)
        def _():
            halo_copy(depth, g, 1, before).start()

    def halo_recv(depth, g):
        @pl.when(has_left)
        def _():
            halo_copy(depth, g, 0, before).wait_recv()

        @pl.when(has_right)
        def _():
            halo_copy(depth, g, 1, after).wait_recv()

    def halo_sent(depth, g):
        @pl.when(has_right)
        def _():
            halo_copy(depth, g, 0, after).wait_send()

        @pl.when(has_left)
        def _():
            halo_copy(depth, g, 1, before).wait_send()

    def field_copy(depth, j):
        return pltpu.make_async_remote_copy(
            src_ref=fsend.at[depth, lax.rem(f + j, nf)],
            dst_ref=fgot.at[depth, j - 1],
            send_sem=fs_sem.at[depth * (nf - 1) + j - 1],
            recv_sem=fr_sem.at[depth * (nf - 1) + j - 1],
            device_id=(lax.rem(f + j, nf), r),
            device_id_type=MESH,
        )

    def raw_copy(depth, p, to, slot, sem):
        return pltpu.make_async_remote_copy(
            src_ref=rsend.at[depth, p],
            dst_ref=rgot.at[depth, slot],
            send_sem=sem,
            recv_sem=rr_sem.at[depth * (nf + 2 * edge) + slot],
            device_id=(p, to),
            device_id_type=MESH,
        )

    def raw_sends(depth, act):
        for j in range(1, nf):
            p = lax.rem(f + j, nf)
            act(raw_copy(depth, p, r, edge + f, rs_sem.at[depth * (nf - 1) + j - 1]))

        @pl.when(has_left)
        def _():
            @pl.when(low)
            def _():
                for p in range(nf):
                    act(raw_copy(depth, p, before, edge + nf + lax.rem(f, edge), es_sem.at[(depth * 2) * nf + p]))

        @pl.when(has_right)
        def _():
            @pl.when(high)
            def _():
                for p in range(nf):
                    slot = lax.rem(f + edge * nf - nf, edge)
                    act(raw_copy(depth, p, after, slot, es_sem.at[(depth * 2 + 1) * nf + p]))

    def raw_recv(depth):
        def wait(slot):
            raw_copy(depth, lax.rem(f + 1, nf), r, slot, rs_sem.at[depth * (nf - 1)]).wait_recv()

        for j in range(1, nf):
            wait(edge + lax.rem(f + j, nf))

        @pl.when(has_left)
        def _():
            for p in range(edge):
                wait(p)

        @pl.when(has_right)
        def _():
            for p in range(edge):
                wait(edge + nf + p)

    def filled(parts):
        count = sum(part.shape[0] for part in parts)
        if count % 8:
            parts = parts + [jnp.zeros((-count % 8, parts[0].shape[1]), parts[0].dtype)]
        return jnp.concatenate(parts, axis=0)

    def widen(value):
        zeros = jnp.zeros((value.shape[0], wide - width), value.dtype)
        return jnp.concatenate([value, zeros], axis=1)

    def step(depth, g):
        taken = jnp.concatenate([table[depth]] * 2, axis=0)
        window = 6 * rows
        parts = []
        for c in range(2):
            part = c if g == 0 else 1 - c
            parts += [halo[depth, 0, g, part], field[depth, g, part], halo[depth, 1, g, part]]
        tall = widen(jnp.concatenate(parts, axis=0).astype(ROLLED))
        for b in range(GROUP):
            turn = (GROUP // 2 - b) % wide
            moved = pltpu.roll(tall, turn, 1) if turn else tall
            shifted[g, b * window : (b + 1) * window, :] = moved.astype(jnp.bfloat16)
        product = jnp.dot(matrix[...], shifted[g], preferred_element_type=jnp.float32)
        block = nv * 2 * rows
        total = None
        for b in range(groups):
            term = product[b * block : (b + 1) * block]
            turn = (-GROUP * (b - groups // 2)) % wide
            term = pltpu.roll(term, turn, 1) if turn else term
            total = term if total is None else total + term
        total = total[:, :width]
        out = total[: 2 * rows]
        for v in range(1, nv):
            out = jnp.where(taken == v, total[v * 2 * rows : (v + 1) * 2 * rows], out)
        return out

    def scatter_fields(depth, chosen):
        sections = [chosen[0][:rows], chosen[0][rows:], chosen[1][rows:], chosen[1][:rows]]
        for p in range(nf):
            piece = [s[p * per : (p + 1) * per] for s in sections]
            piece = filled(piece)
            piece = jnp.concatenate([piece[:, : width // 2], piece[:, width // 2 :]], axis=0)
            fsend[depth, p] = piece.astype(jnp.bfloat16)
        for j in range(1, nf):
            field_copy(depth, j).start()

    def correlate(depth):
        for j in range(1, nf):
            field_copy(depth, j).wait_recv()
        downs, ups = [], []
        for j in range(nf):
            piece = fsend[depth, f] if j == 0 else fgot[depth, j - 1]
            piece = piece.astype(jnp.float32)
            tile = piece.shape[0] // 2
            piece = jnp.concatenate([piece[:tile], piece[tile:]], axis=1)
            downs.append(piece[: 2 * per])
            ups.append(piece[2 * per : 4 * per])
        down = widen(jnp.concatenate(downs, axis=0))
        up = widen(jnp.concatenate(ups, axis=0))
        shift = noff // 2
        for lag in range(noff):
            offset = lag - shift
            turn = (-2 * offset) % wide
            terms = down * (pltpu.roll(up, turn, 1) if turn else up)
            total = terms[:8]
            for i in range(1, terms.shape[0] // 8):
                total = total + terms[8 * i : 8 * i + 8]
            turn = offset % wide
            total = (pltpu.roll(total, turn, 1) if turn else total)[:, :width]
            raw = total[:per]
            for i in range(1, 8 // per):
                raw = raw + total[i * per : (i + 1) * per]
            by_lag[lag] = filled([raw[:, : width // 2], raw[:, width // 2 :]])
        for p in range(nf):
            rsend[depth, p] = filled([by_lag[lags[p * kper + k]][: 2 * per] for k in range(kper)])
        raw_sends(depth, lambda copy: copy.start())
        rgot[depth, edge + f] = rsend[depth, f]

    def filter_images(depth):
        raw_recv(depth)
        pieces = [rgot[depth, s] for s in range(nf + 2 * edge)]
        for k in range(kper):
            left, right = (
                jnp.concatenate([piece[at : at + per] for piece in pieces], axis=0)
                for at in (2 * per * k, 2 * per * k + per)
            )
            plane[k] = widen(jnp.concatenate([left, right], axis=1))
        for k in range(kper):
            for top in range(0, rows, 8):
                columns = [None] * ofilt
                for a in range(ofilt):
                    lines = plane[k, top + a : top + a + 8, :]
                    for b in range(ofilt):
                        term = ofilters[a, k, b] * lines
                        columns[b] = term if a == 0 else columns[b] + term
                total = None
                for b in range(ofilt):
                    turn = (ohalf - b) % wide
                    column = pltpu.roll(columns[b], turn, 1) if turn else columns[b]
                    column = column[:, :width]
                    total = column if total is None else total + column
                image[depth, k, top : top + 8, :] = total

    halo_start(0, 0)
    halo_start(0, 1)

    matrix[...] = filter_matrix(taps, filt, rows)
    spare = shifted.shape[1] - GROUP * 6 * rows
    if spare:
        for g in range(2):
            shifted[g, GROUP * 6 * rows :, :] = jnp.zeros((spare, wide), jnp.bfloat16)

    for depth in range(depths):
        chosen = []
        for g in range(2):
            if depth == 0:
                loads[g].wait()
                if g == 0:
                    loads[2].wait()
            halo_recv(depth, g)
            out = step(depth, g)
            if depth + 1 < depths:
                field[depth + 1, g, 0] = out[g * rows : (g + 1) * rows].astype(jnp.bfloat16)
                field[depth + 1, g, 1] = out[(1 - g) * rows : (2 - g) * rows].astype(jnp.bfloat16)
                halo_start(depth + 1, g)
            chosen.append(out)
        scatter_fields(depth, chosen)
    for depth in range(depths):
        correlate(depth)
    for depth in range(depths):
        filter_images(depth)
    for depth in range(depths):
        for g in range(2):
            halo_sent(depth, g)
        for j in range(1, nf):
            field_copy(depth, j).wait_send()
        raw_sends(depth, lambda copy: copy.wait_send())


def body(nf, nr, source, receiver, filters, table_index, lags, offset_filters):
    depths, rows, width = table_index.shape
    noff = lags.shape[0]
    kper, ofilt, _ = offset_filters.shape
    per = rows // nf
    edge = (ofilt - 1) // 2 // per
    wide = width + LANES
    nv, filt = filters.shape[1], filters.shape[3]
    taps = filters.transpose(0, 1, 2, 4, 3).reshape(nv * 2, filt, filt)
    taps = jnp.pad(taps, ((0, 0), (0, -filt % 32), (0, -filt % LANES)))
    groups = -(-filt // GROUP)
    contracted = -(-(GROUP * 6 * rows) // LANES) * LANES
    piece = -(-4 * per // 8) * 16
    image_piece = -(-2 * per * kper // 8) * 8
    half = width // 2
    vmem = pl.BlockSpec(memory_space=pltpu.VMEM)
    far = pl.BlockSpec(memory_space=pl.ANY)
    smem = pl.BlockSpec(memory_space=pltpu.SMEM)
    dma = pltpu.SemaphoreType.DMA
    return pl.pallas_call(
        functools.partial(kernel, nf, nr, filt),
        out_shape=jax.ShapeDtypeStruct((depths, kper, rows, width), jnp.float32),
        in_specs=[far, far, vmem, far, smem, smem],
        out_specs=vmem,
        scratch_shapes=[
            pltpu.VMEM(table_index.shape, jnp.int32),
            pltpu.VMEM((groups * nv * 2 * rows, contracted), jnp.bfloat16),
            pltpu.VMEM((2, contracted, wide), jnp.bfloat16),
            pltpu.VMEM((depths, 2, 2, rows, width), jnp.bfloat16),
            pltpu.VMEM((depths, 2, 2, 2, rows, width), jnp.bfloat16),
            pltpu.VMEM((depths, nf, piece, half), jnp.bfloat16),
            pltpu.VMEM((depths, nf - 1, piece, half), jnp.bfloat16),
            pltpu.VMEM((noff, -(-2 * per // 8) * 8, half), jnp.float32),
            pltpu.VMEM((depths, nf, image_piece, half), jnp.float32),
            pltpu.VMEM((depths, nf + 2 * edge, image_piece, half), jnp.float32),
            pltpu.VMEM((kper, rows + ofilt - 1, wide), jnp.float32),
            dma((depths * 4,)),
            dma((depths * 4,)),
            dma((depths * (nf - 1),)),
            dma((depths * (nf - 1),)),
            dma((depths * (nf - 1),)),
            dma((depths * (nf + 2 * edge),)),
            dma((depths * 2 * nf,)),
            dma((3,)),
        ],
        compiler_params=pltpu.CompilerParams(
            collective_id=0, has_side_effects=True, vmem_limit_bytes=60 * 1024 * 1024
        ),
    )(source, receiver, taps, table_index, lags, offset_filters.transpose(1, 0, 2))


def solution(mesh):
    in_specs = (
        P("freq", None, "row", None),
        P("freq", None, "row", None),
        P("freq", None, None, None, None),
        P(None, "row", None),
        P(),
        P("freq", None, None),
    )
    out_specs = P(None, "freq", "row", None)
    return jax.shard_map(
        functools.partial(body, mesh.shape["freq"], mesh.shape["row"]),
        mesh=mesh,
        in_specs=in_specs,
        out_specs=out_specs,
        check_vma=False,
    )
```

```python
import functools

import jax
import jax.numpy as jnp
from jax import lax
from jax.experimental import pallas as pl
from jax.experimental.pallas import tpu as pltpu
from jax.sharding import PartitionSpec as P

MESH = pl.DeviceIdType.MESH
GROUP = 5
LANES = 128
ROLLED = jnp.bfloat16


def filter_matrix(taps, filt, rows):
    nv = taps.shape[0] // 2
    window = 3 * rows
    lead = rows - (filt - 1) // 2
    groups = -(-filt // GROUP)
    depth = -(-(GROUP * 2 * window) // LANES) * LANES
    at = lax.broadcasted_iota(jnp.int32, (taps.shape[2], depth), 1)
    first = lax.broadcasted_iota(jnp.int32, (taps.shape[2], depth), 0)
    section = lax.div(at, window)
    place = (at - section * window == first + lead) & (section < 2 * GROUP)
    place = place.astype(jnp.float32).astype(jnp.bfloat16)
    columns = taps.shape[1]
    first, section = first[:columns], section[:columns]
    kept = lax.rem(first, GROUP) == lax.div(section, 2)
    real_in = lax.rem(section, 2) == 0
    group_of = lax.div(lax.broadcasted_iota(jnp.int32, (groups * rows, columns), 0), rows)
    spread = lax.div(lax.broadcasted_iota(jnp.int32, (groups * rows, columns), 1), GROUP) == group_of
    spread = spread.astype(jnp.float32).astype(jnp.bfloat16)
    blocks = []
    for v in range(nv):
        real, imag = (
            jnp.where(kept, jnp.dot(taps[2 * v + i], place, preferred_element_type=jnp.float32), 0.0)
            for i in range(2)
        )
        for out in (jnp.where(real_in, real, -imag), jnp.where(real_in, imag, real)):
            blocks.append(jnp.dot(spread, out.astype(jnp.bfloat16), preferred_element_type=jnp.float32))
    tall = jnp.concatenate(
        [block[g * rows : (g + 1) * rows] for g in range(groups) for block in blocks], axis=0
    )
    row_ids = lax.rem(lax.broadcasted_iota(jnp.int32, tall.shape, 0), rows)
    move = 1
    while move < rows:
        tall = jnp.where(row_ids & move != 0, pltpu.roll(tall, move, 1), tall)
        move *= 2
    return tall.astype(jnp.bfloat16)


def kernel(
    nf,
    nr,
    filt,
    source,
    receiver,
    taps,
    index,
    lags,
    ofilters,
    image,
    matrix,
    shifted,
    field,
    halo,
    fsend,
    fgot,
    by_lag,
    rsend,
    rgot,
    plane,
    hs_sem,
    hr_sem,
    fs_sem,
    fr_sem,
    rs_sem,
    rr_sem,
    es_sem,
):
    depths, rows, width = index.shape
    noff = lags.shape[0]
    ofilt, kper, _ = ofilters.shape
    ohalf = (ofilt - 1) // 2
    per = rows // nf
    edge = ohalf // per
    wide = width + LANES
    groups = -(-filt // GROUP)
    nv = matrix.shape[0] // (groups * 2 * rows)

    f = lax.axis_index("freq")
    r = lax.axis_index("row")
    before, after = lax.rem(r + nr - 1, nr), lax.rem(r + 1, nr)
    has_left = r > 0
    has_right = r < nr - 1
    low = f < edge
    high = f >= nf - edge

    barrier = pltpu.get_barrier_semaphore()

    def greet(ff, rr):
        pl.semaphore_signal(barrier, inc=1, device_id=(ff, rr), device_id_type=MESH)

    @pl.when(has_left)
    def _():
        for p in range(nf - edge, nf):
            greet(p, before)

        @pl.when(f < nf - edge)
        def _():
            greet(f, before)

    @pl.when(has_right)
    def _():
        for p in range(edge):
            greet(p, after)

        @pl.when(f >= edge)
        def _():
            greet(f, after)

    for j in range(1, nf):
        greet(lax.rem(f + j, nf), r)

    def clear(side, first):
        for depth in range(depths):
            for g in range(2):
                for c in range(2):
                    halo[depth, side, g, c] = jnp.zeros((rows, width), halo.dtype)
            for p in range(edge):
                rgot[depth, first + p] = jnp.zeros(rgot.shape[2:], rgot.dtype)

    @pl.when(r < 1)
    def _():
        clear(0, 0)

    @pl.when(r >= nr - 1)
    def _():
        clear(1, edge + nf)

    pl.semaphore_wait(
        barrier,
        nf
        - 1
        + jnp.where(has_left, jnp.where(low, nf, 1), 0)
        + jnp.where(has_right, jnp.where(high, nf, 1), 0),
    )

    def halo_copy(depth, g, side, to):
        src = (source, receiver)[g].at[0] if depth == 0 else field.at[depth - 1, g]
        return pltpu.make_async_remote_copy(
            src_ref=src,
            dst_ref=halo.at[depth, side, g],
            send_sem=hs_sem.at[(depth * 2 + side) * 2 + g],
            recv_sem=hr_sem.at[(depth * 2 + side) * 2 + g],
            device_id=(f, to),
            device_id_type=MESH,
        )

    def halo_start(depth, g):
        @pl.when(has_right)
        def _():
            halo_copy(depth, g, 0, after).start()

        @pl.when(has_left)
        def _():
            halo_copy(depth, g, 1, before).start()

    def halo_recv(depth, g):
        @pl.when(has_left)
        def _():
            halo_copy(depth, g, 0, before).wait_recv()

        @pl.when(has_right)
        def _():
            halo_copy(depth, g, 1, after).wait_recv()

    def halo_sent(depth, g):
        @pl.when(has_right)
        def _():
            halo_copy(depth, g, 0, after).wait_send()

        @pl.when(has_left)
        def _():
            halo_copy(depth, g, 1, before).wait_send()

    def field_copy(depth, j):
        return pltpu.make_async_remote_copy(
            src_ref=fsend.at[depth, lax.rem(f + j, nf)],
            dst_ref=fgot.at[depth, j - 1],
            send_sem=fs_sem.at[depth * (nf - 1) + j - 1],
            recv_sem=fr_sem.at[depth * (nf - 1) + j - 1],
            device_id=(lax.rem(f + j, nf), r),
            device_id_type=MESH,
        )

    def raw_copy(depth, p, to, slot, sem):
        return pltpu.make_async_remote_copy(
            src_ref=rsend.at[depth, p],
            dst_ref=rgot.at[depth, slot],
            send_sem=sem,
            recv_sem=rr_sem.at[depth * (nf + 2 * edge) + slot],
            device_id=(p, to),
            device_id_type=MESH,
        )

    def raw_sends(depth, act):
        @pl.when(has_left)
        def _():
            @pl.when(low)
            def _():
                for p in range(nf):
                    act(raw_copy(depth, p, before, edge + nf + lax.rem(f, edge), es_sem.at[(depth * 2) * nf + p]))

        @pl.when(has_right)
        def _():
            @pl.when(high)
            def _():
                for p in range(nf):
                    slot = lax.rem(f + edge * nf - nf, edge)
                    act(raw_copy(depth, p, after, slot, es_sem.at[(depth * 2 + 1) * nf + p]))

        for j in range(1, nf):
            p = lax.rem(f + j, nf)
            act(raw_copy(depth, p, r, edge + f, rs_sem.at[depth * (nf - 1) + j - 1]))

    def raw_recv(depth):
        def wait(slot):
            raw_copy(depth, lax.rem(f + 1, nf), r, slot, rs_sem.at[depth * (nf - 1)]).wait_recv()

        for j in range(1, nf):
            wait(edge + lax.rem(f + j, nf))

        @pl.when(has_left)
        def _():
            for p in range(edge):
                wait(p)

        @pl.when(has_right)
        def _():
            for p in range(edge):
                wait(edge + nf + p)

    def filled(parts):
        count = sum(part.shape[0] for part in parts)
        if count % 8:
            parts = parts + [jnp.zeros((-count % 8, parts[0].shape[1]), parts[0].dtype)]
        return jnp.concatenate(parts, axis=0)

    def widen(value):
        zeros = jnp.zeros((value.shape[0], wide - width), value.dtype)
        return jnp.concatenate([value, zeros], axis=1)

    def step(depth, g):
        taken = jnp.concatenate([index[depth]] * 2, axis=0)
        window = 6 * rows
        parts = []
        for c in range(2):
            part = c if g == 0 else 1 - c
            own = (source, receiver)[g][0, part] if depth == 0 else field[depth - 1, g, part]
            parts += [halo[depth, 0, g, part], own, halo[depth, 1, g, part]]
        tall = widen(jnp.concatenate(parts, axis=0).astype(ROLLED))
        for b in range(GROUP):
            turn = (GROUP // 2 - b) % wide
            moved = pltpu.roll(tall, turn, 1) if turn else tall
            shifted[g, b * window : (b + 1) * window, :] = moved.astype(jnp.bfloat16)
        product = jnp.dot(matrix[...], shifted[g], preferred_element_type=jnp.float32)
        block = nv * 2 * rows
        total = None
        for b in range(groups):
            term = product[b * block : (b + 1) * block]
            turn = (-GROUP * (b - groups // 2)) % wide
            term = pltpu.roll(term, turn, 1) if turn else term
            total = term if total is None else total + term
        total = total[:, :width]
        out = total[: 2 * rows]
        for v in range(1, nv):
            out = jnp.where(taken == v, total[v * 2 * rows : (v + 1) * 2 * rows], out)
        return out

    def scatter_fields(depth, chosen):
        sections = [chosen[0][:rows], chosen[0][rows:], chosen[1][rows:], chosen[1][:rows]]
        for p in range(nf):
            piece = [s[p * per : (p + 1) * per] for s in sections]
            piece = filled(piece)
            piece = jnp.concatenate([piece[:, : width // 2], piece[:, width // 2 :]], axis=0)
            fsend[depth, p] = piece.astype(jnp.bfloat16)
        for j in range(1, nf):
            field_copy(depth, j).start()

    def correlate(depth):
        for j in range(1, nf):
            field_copy(depth, j).wait_recv()
        downs, ups = [], []
        for j in range(nf):
            piece = fsend[depth, f] if j == 0 else fgot[depth, j - 1]
            piece = piece.astype(jnp.float32)
            tile = piece.shape[0] // 2
            piece = jnp.concatenate([piece[:tile], piece[tile:]], axis=1)
            downs.append(piece[: 2 * per])
            ups.append(piece[2 * per : 4 * per])
        down = widen(jnp.concatenate(downs, axis=0))
        up = widen(jnp.concatenate(ups, axis=0))
        shift = noff // 2
        for lag in range(noff):
            offset = lag - shift
            turn = (-2 * offset) % wide
            terms = down * (pltpu.roll(up, turn, 1) if turn else up)
            total = terms[:8]
            for i in range(1, terms.shape[0] // 8):
                total = total + terms[8 * i : 8 * i + 8]
            turn = offset % wide
            total = (pltpu.roll(total, turn, 1) if turn else total)[:, :width]
            raw = total[:per]
            for i in range(1, 8 // per):
                raw = raw + total[i * per : (i + 1) * per]
            by_lag[lag] = filled([raw[:, : width // 2], raw[:, width // 2 :]])
        for p in range(nf):
            rsend[depth, p] = filled([by_lag[lags[p * kper + k]][: 2 * per] for k in range(kper)])
        raw_sends(depth, lambda copy: copy.start())
        rgot[depth, edge + f] = rsend[depth, f]

    def filter_images(depth):
        raw_recv(depth)
        pieces = [rgot[depth, s] for s in range(nf + 2 * edge)]
        for k in range(kper):
            left, right = (
                jnp.concatenate([piece[at : at + per] for piece in pieces], axis=0)
                for at in (2 * per * k, 2 * per * k + per)
            )
            plane[k] = widen(jnp.concatenate([left, right], axis=1))
        for k in range(kper):
            for top in range(0, rows, 8):
                columns = [None] * ofilt
                for a in range(ofilt):
                    lines = plane[k, top + a : top + a + 8, :]
                    for b in range(ofilt):
                        term = ofilters[a, k, b] * lines
                        columns[b] = term if a == 0 else columns[b] + term
                total = None
                for b in range(ofilt):
                    turn = (ohalf - b) % wide
                    column = pltpu.roll(columns[b], turn, 1) if turn else columns[b]
                    column = column[:, :width]
                    total = column if total is None else total + column
                image[depth, k, top : top + 8, :] = total

    halo_start(0, 0)
    halo_start(0, 1)

    matrix[...] = filter_matrix(taps, filt, rows)
    spare = shifted.shape[1] - GROUP * 6 * rows
    if spare:
        for g in range(2):
            shifted[g, GROUP * 6 * rows :, :] = jnp.zeros((spare, wide), jnp.bfloat16)

    for depth in range(depths):
        chosen = []
        for g in range(2):
            halo_recv(depth, g)
            out = step(depth, g)
            if depth + 1 < depths:
                field[depth, g, 0] = out[g * rows : (g + 1) * rows].astype(jnp.bfloat16)
                field[depth, g, 1] = out[(1 - g) * rows : (2 - g) * rows].astype(jnp.bfloat16)
                halo_start(depth + 1, g)
            chosen.append(out)
        scatter_fields(depth, chosen)
    for depth in range(depths):
        correlate(depth)
    for depth in range(depths):
        filter_images(depth)
    for depth in range(depths):
        for g in range(2):
            halo_sent(depth, g)
        for j in range(1, nf):
            field_copy(depth, j).wait_send()
        raw_sends(depth, lambda copy: copy.wait_send())


def body(nf, nr, source, receiver, filters, table_index, lags, offset_filters):
    depths, rows, width = table_index.shape
    noff = lags.shape[0]
    kper, ofilt, _ = offset_filters.shape
    per = rows // nf
    edge = (ofilt - 1) // 2 // per
    wide = width + LANES
    nv, filt = filters.shape[1], filters.shape[3]
    taps = filters.transpose(0, 1, 2, 4, 3).reshape(nv * 2, filt, filt)
    taps = jnp.pad(taps, ((0, 0), (0, -filt % 32), (0, -filt % LANES)))
    groups = -(-filt // GROUP)
    contracted = -(-(GROUP * 6 * rows) // LANES) * LANES
    piece = -(-4 * per // 8) * 16
    image_piece = -(-2 * per * kper // 8) * 8
    half = width // 2
    vmem = pl.BlockSpec(memory_space=pltpu.VMEM)
    smem = pl.BlockSpec(memory_space=pltpu.SMEM)
    dma = pltpu.SemaphoreType.DMA
    return pl.pallas_call(
        functools.partial(kernel, nf, nr, filt),
        out_shape=jax.ShapeDtypeStruct((depths, kper, rows, width), jnp.float32),
        in_specs=[vmem, vmem, vmem, vmem, smem, smem],
        out_specs=vmem,
        scratch_shapes=[
            pltpu.VMEM((groups * nv * 2 * rows, contracted), jnp.bfloat16),
            pltpu.VMEM((2, contracted, wide), jnp.bfloat16),
            pltpu.VMEM((depths, 2, 2, rows, width), jnp.bfloat16),
            pltpu.VMEM((depths, 2, 2, 2, rows, width), jnp.bfloat16),
            pltpu.VMEM((depths, nf, piece, half), jnp.bfloat16),
            pltpu.VMEM((depths, nf - 1, piece, half), jnp.bfloat16),
            pltpu.VMEM((noff, -(-2 * per // 8) * 8, half), jnp.float32),
            pltpu.VMEM((depths, nf, image_piece, half), jnp.float32),
            pltpu.VMEM((depths, nf + 2 * edge, image_piece, half), jnp.float32),
            pltpu.VMEM((kper, rows + ofilt - 1, wide), jnp.float32),
            dma((depths * 4,)),
            dma((depths * 4,)),
            dma((depths * (nf - 1),)),
            dma((depths * (nf - 1),)),
            dma((depths * (nf - 1),)),
            dma((depths * (nf + 2 * edge),)),
            dma((depths * 2 * nf,)),
        ],
        compiler_params=pltpu.CompilerParams(
            collective_id=0, has_side_effects=True, vmem_limit_bytes=48 * 1024 * 1024
        ),
    )(source, receiver, taps, table_index, lags, offset_filters.transpose(1, 0, 2))


def solution(mesh):
    in_specs = (
        P("freq", None, "row", None),
        P("freq", None, "row", None),
        P("freq", None, None, None, None),
        P(None, "row", None),
        P(),
        P("freq", None, None),
    )
    out_specs = P(None, "freq", "row", None)
    return jax.shard_map(
        functools.partial(body, mesh.shape["freq"], mesh.shape["row"]),
        mesh=mesh,
        in_specs=in_specs,
        out_specs=out_specs,
        check_vma=False,
    )
```

```python
import functools

import jax
import jax.numpy as jnp
from jax import lax
from jax.experimental import pallas as pl
from jax.experimental.pallas import tpu as pltpu
from jax.sharding import PartitionSpec as P

MESH = pl.DeviceIdType.MESH
GROUP = 5
LANES = 128
ROLLED = jnp.bfloat16


def filter_matrix(taps, filt, rows):
    nv = taps.shape[0] // 2
    window = 3 * rows
    lead = rows - (filt - 1) // 2
    groups = -(-filt // GROUP)
    depth = -(-(GROUP * 2 * window) // LANES) * LANES
    at = lax.broadcasted_iota(jnp.int32, (taps.shape[2], depth), 1)
    first = lax.broadcasted_iota(jnp.int32, (taps.shape[2], depth), 0)
    section = lax.div(at, window)
    place = (at - section * window == first + lead) & (section < 2 * GROUP)
    place = place.astype(jnp.float32).astype(jnp.bfloat16)
    columns = taps.shape[1]
    first, section = first[:columns], section[:columns]
    kept = lax.rem(first, GROUP) == lax.div(section, 2)
    real_in = lax.rem(section, 2) == 0
    group_of = lax.div(lax.broadcasted_iota(jnp.int32, (groups * rows, columns), 0), rows)
    spread = lax.div(lax.broadcasted_iota(jnp.int32, (groups * rows, columns), 1), GROUP) == group_of
    spread = spread.astype(jnp.float32).astype(jnp.bfloat16)
    blocks = []
    for v in range(nv):
        real, imag = (
            jnp.where(kept, jnp.dot(taps[2 * v + i], place, preferred_element_type=jnp.float32), 0.0)
            for i in range(2)
        )
        for out in (jnp.where(real_in, real, -imag), jnp.where(real_in, imag, real)):
            blocks.append(jnp.dot(spread, out.astype(jnp.bfloat16), preferred_element_type=jnp.float32))
    tall = jnp.concatenate(
        [block[g * rows : (g + 1) * rows] for g in range(groups) for block in blocks], axis=0
    )
    row_ids = lax.rem(lax.broadcasted_iota(jnp.int32, tall.shape, 0), rows)
    move = 1
    while move < rows:
        tall = jnp.where(row_ids & move != 0, pltpu.roll(tall, move, 1), tall)
        move *= 2
    return tall.astype(jnp.bfloat16)


def kernel(
    nf,
    nr,
    filt,
    source,
    receiver,
    taps,
    index,
    lags,
    ofilters,
    image,
    matrix,
    shifted,
    field,
    halo,
    fsend,
    fgot,
    by_lag,
    rsend,
    rgot,
    plane,
    hs_sem,
    hr_sem,
    fs_sem,
    fr_sem,
    rs_sem,
    rr_sem,
    es_sem,
):
    depths, rows, width = index.shape
    noff = lags.shape[0]
    ofilt, kper, _ = ofilters.shape
    ohalf = (ofilt - 1) // 2
    per = rows // nf
    edge = ohalf // per
    wide = width + LANES
    groups = -(-filt // GROUP)
    nv = matrix.shape[0] // (groups * 2 * rows)

    f = lax.axis_index("freq")
    r = lax.axis_index("row")
    before, after = lax.rem(r + nr - 1, nr), lax.rem(r + 1, nr)
    has_left = r > 0
    has_right = r < nr - 1
    low = f < edge
    high = f >= nf - edge

    barrier = pltpu.get_barrier_semaphore()

    def greet(ff, rr):
        pl.semaphore_signal(barrier, inc=1, device_id=(ff, rr), device_id_type=MESH)

    @pl.when(has_left)
    def _():
        for p in range(nf - edge, nf):
            greet(p, before)

        @pl.when(f < nf - edge)
        def _():
            greet(f, before)

    @pl.when(has_right)
    def _():
        for p in range(edge):
            greet(p, after)

        @pl.when(f >= edge)
        def _():
            greet(f, after)

    for j in range(1, nf):
        greet(lax.rem(f + j, nf), r)

    def clear(side, first):
        for depth in range(depths):
            for g in range(2):
                for c in range(2):
                    halo[depth, side, g, c] = jnp.zeros((rows, width), halo.dtype)
            for p in range(edge):
                rgot[depth, first + p] = jnp.zeros(rgot.shape[2:], rgot.dtype)

    @pl.when(r < 1)
    def _():
        clear(0, 0)

    @pl.when(r >= nr - 1)
    def _():
        clear(1, edge + nf)

    pl.semaphore_wait(
        barrier,
        nf
        - 1
        + jnp.where(has_left, jnp.where(low, nf, 1), 0)
        + jnp.where(has_right, jnp.where(high, nf, 1), 0),
    )

    def halo_copy(depth, g, side, to):
        src = (source, receiver)[g].at[0] if depth == 0 else field.at[depth - 1, g]
        return pltpu.make_async_remote_copy(
            src_ref=src,
            dst_ref=halo.at[depth, side, g],
            send_sem=hs_sem.at[(depth * 2 + side) * 2 + g],
            recv_sem=hr_sem.at[(depth * 2 + side) * 2 + g],
            device_id=(f, to),
            device_id_type=MESH,
        )

    def halo_start(depth, g):
        @pl.when(has_right)
        def _():
            halo_copy(depth, g, 0, after).start()

        @pl.when(has_left)
        def _():
            halo_copy(depth, g, 1, before).start()

    def halo_recv(depth, g):
        @pl.when(has_left)
        def _():
            halo_copy(depth, g, 0, before).wait_recv()

        @pl.when(has_right)
        def _():
            halo_copy(depth, g, 1, after).wait_recv()

    def halo_sent(depth, g):
        @pl.when(has_right)
        def _():
            halo_copy(depth, g, 0, after).wait_send()

        @pl.when(has_left)
        def _():
            halo_copy(depth, g, 1, before).wait_send()

    def field_copy(depth, j):
        return pltpu.make_async_remote_copy(
            src_ref=fsend.at[depth, lax.rem(f + j, nf)],
            dst_ref=fgot.at[depth, j - 1],
            send_sem=fs_sem.at[depth * (nf - 1) + j - 1],
            recv_sem=fr_sem.at[depth * (nf - 1) + j - 1],
            device_id=(lax.rem(f + j, nf), r),
            device_id_type=MESH,
        )

    def raw_copy(depth, p, to, slot, sem):
        return pltpu.make_async_remote_copy(
            src_ref=rsend.at[depth, p],
            dst_ref=rgot.at[depth, slot],
            send_sem=sem,
            recv_sem=rr_sem.at[depth * (nf + 2 * edge) + slot],
            device_id=(p, to),
            device_id_type=MESH,
        )

    def raw_sends(depth, act):
        @pl.when(has_left)
        def _():
            @pl.when(low)
            def _():
                for p in range(nf):
                    act(raw_copy(depth, p, before, edge + nf + lax.rem(f, edge), es_sem.at[(depth * 2) * nf + p]))

        @pl.when(has_right)
        def _():
            @pl.when(high)
            def _():
                for p in range(nf):
                    slot = lax.rem(f + edge * nf - nf, edge)
                    act(raw_copy(depth, p, after, slot, es_sem.at[(depth * 2 + 1) * nf + p]))

        for j in range(1, nf):
            p = lax.rem(f + j, nf)
            act(raw_copy(depth, p, r, edge + f, rs_sem.at[depth * (nf - 1) + j - 1]))

    def raw_recv(depth):
        def wait(slot):
            raw_copy(depth, lax.rem(f + 1, nf), r, slot, rs_sem.at[depth * (nf - 1)]).wait_recv()

        for j in range(1, nf):
            wait(edge + lax.rem(f + j, nf))

        @pl.when(has_left)
        def _():
            for p in range(edge):
                wait(p)

        @pl.when(has_right)
        def _():
            for p in range(edge):
                wait(edge + nf + p)

    def filled(parts):
        count = sum(part.shape[0] for part in parts)
        if count % 8:
            parts = parts + [jnp.zeros((-count % 8, parts[0].shape[1]), parts[0].dtype)]
        return jnp.concatenate(parts, axis=0)

    def widen(value):
        zeros = jnp.zeros((value.shape[0], wide - width), value.dtype)
        return jnp.concatenate([value, zeros], axis=1)

    def step(depth, g):
        taken = jnp.concatenate([index[depth]] * 2, axis=0)
        window = 6 * rows
        parts = []
        for c in range(2):
            part = c if g == 0 else 1 - c
            own = (source, receiver)[g][0, part] if depth == 0 else field[depth - 1, g, part]
            parts += [halo[depth, 0, g, part], own, halo[depth, 1, g, part]]
        tall = widen(jnp.concatenate(parts, axis=0).astype(ROLLED))
        for b in range(GROUP):
            turn = (GROUP // 2 - b) % wide
            moved = pltpu.roll(tall, turn, 1) if turn else tall
            shifted[g, b * window : (b + 1) * window, :] = moved.astype(jnp.bfloat16)
        product = jnp.dot(matrix[...], shifted[g], preferred_element_type=jnp.float32)
        block = nv * 2 * rows
        total = None
        for b in range(groups):
            term = product[b * block : (b + 1) * block]
            turn = (-GROUP * (b - groups // 2)) % wide
            term = pltpu.roll(term, turn, 1) if turn else term
            total = term if total is None else total + term
        total = total[:, :width]
        out = total[: 2 * rows]
        for v in range(1, nv):
            out = jnp.where(taken == v, total[v * 2 * rows : (v + 1) * 2 * rows], out)
        return out

    def scatter_fields(depth, chosen):
        sections = [chosen[0][:rows], chosen[0][rows:], chosen[1][rows:], chosen[1][:rows]]
        for p in range(nf):
            piece = [s[p * per : (p + 1) * per] for s in sections]
            piece = filled(piece)
            piece = jnp.concatenate([piece[:, : width // 2], piece[:, width // 2 :]], axis=0)
            fsend[depth, p] = piece.astype(jnp.bfloat16)
        for j in range(1, nf):
            field_copy(depth, j).start()

    def correlate(depth):
        for j in range(1, nf):
            field_copy(depth, j).wait_recv()
        downs, ups = [], []
        for j in range(nf):
            piece = fsend[depth, f] if j == 0 else fgot[depth, j - 1]
            piece = piece.astype(jnp.float32)
            tile = piece.shape[0] // 2
            piece = jnp.concatenate([piece[:tile], piece[tile:]], axis=1)
            downs.append(piece[: 2 * per])
            ups.append(piece[2 * per : 4 * per])
        down = widen(jnp.concatenate(downs, axis=0))
        up = widen(jnp.concatenate(ups, axis=0))
        shift = noff // 2
        for lag in range(noff):
            offset = lag - shift
            turn = (-2 * offset) % wide
            terms = down * (pltpu.roll(up, turn, 1) if turn else up)
            total = terms[:8]
            for i in range(1, terms.shape[0] // 8):
                total = total + terms[8 * i : 8 * i + 8]
            turn = offset % wide
            total = (pltpu.roll(total, turn, 1) if turn else total)[:, :width]
            raw = total[:per]
            for i in range(1, 8 // per):
                raw = raw + total[i * per : (i + 1) * per]
            by_lag[lag] = filled([raw[:, : width // 2], raw[:, width // 2 :]])
        for p in range(nf):
            rsend[depth, p] = filled([by_lag[lags[p * kper + k]][: 2 * per] for k in range(kper)])
        raw_sends(depth, lambda copy: copy.start())
        rgot[depth, edge + f] = rsend[depth, f]

    def filter_images(depth):
        raw_recv(depth)
        pieces = [rgot[depth, s] for s in range(nf + 2 * edge)]
        for k in range(kper):
            left, right = (
                jnp.concatenate([piece[at : at + per] for piece in pieces], axis=0)
                for at in (2 * per * k, 2 * per * k + per)
            )
            plane[k] = widen(jnp.concatenate([left, right], axis=1))
        for k in range(kper):
            for top in range(0, rows, 8):
                columns = [None] * ofilt
                for a in range(ofilt):
                    lines = plane[k, top + a : top + a + 8, :]
                    for b in range(ofilt):
                        term = ofilters[a, k, b] * lines
                        columns[b] = term if a == 0 else columns[b] + term
                total = None
                for b in range(ofilt):
                    turn = (ohalf - b) % wide
                    column = pltpu.roll(columns[b], turn, 1) if turn else columns[b]
                    column = column[:, :width]
                    total = column if total is None else total + column
                image[depth, k, top : top + 8, :] = total

    halo_start(0, 0)
    halo_start(0, 1)

    matrix[...] = filter_matrix(taps, filt, rows)
    spare = shifted.shape[1] - GROUP * 6 * rows
    if spare:
        for g in range(2):
            shifted[g, GROUP * 6 * rows :, :] = jnp.zeros((spare, wide), jnp.bfloat16)

    for depth in range(depths):
        chosen = []
        for g in range(2):
            halo_recv(depth, g)
            out = step(depth, g)
            if depth + 1 < depths:
                field[depth, g, 0] = out[g * rows : (g + 1) * rows].astype(jnp.bfloat16)
                field[depth, g, 1] = out[(1 - g) * rows : (2 - g) * rows].astype(jnp.bfloat16)
                halo_start(depth + 1, g)
            chosen.append(out)
            if g == 0 and depth:
                correlate(depth - 1)
        scatter_fields(depth, chosen)
        if depth:
            filter_images(depth - 1)
    correlate(depths - 1)
    filter_images(depths - 1)
    for depth in range(depths):
        for g in range(2):
            halo_sent(depth, g)
        for j in range(1, nf):
            field_copy(depth, j).wait_send()
        raw_sends(depth, lambda copy: copy.wait_send())


def body(nf, nr, source, receiver, filters, table_index, lags, offset_filters):
    depths, rows, width = table_index.shape
    noff = lags.shape[0]
    kper, ofilt, _ = offset_filters.shape
    per = rows // nf
    edge = (ofilt - 1) // 2 // per
    wide = width + LANES
    nv, filt = filters.shape[1], filters.shape[3]
    taps = filters.transpose(0, 1, 2, 4, 3).reshape(nv * 2, filt, filt)
    taps = jnp.pad(taps, ((0, 0), (0, -filt % 32), (0, -filt % LANES)))
    groups = -(-filt // GROUP)
    contracted = -(-(GROUP * 6 * rows) // LANES) * LANES
    piece = -(-4 * per // 8) * 16
    image_piece = -(-2 * per * kper // 8) * 8
    half = width // 2
    vmem = pl.BlockSpec(memory_space=pltpu.VMEM)
    smem = pl.BlockSpec(memory_space=pltpu.SMEM)
    dma = pltpu.SemaphoreType.DMA
    return pl.pallas_call(
        functools.partial(kernel, nf, nr, filt),
        out_shape=jax.ShapeDtypeStruct((depths, kper, rows, width), jnp.float32),
        in_specs=[vmem, vmem, vmem, vmem, smem, smem],
        out_specs=vmem,
        scratch_shapes=[
            pltpu.VMEM((groups * nv * 2 * rows, contracted), jnp.bfloat16),
            pltpu.VMEM((2, contracted, wide), jnp.bfloat16),
            pltpu.VMEM((depths, 2, 2, rows, width), jnp.bfloat16),
            pltpu.VMEM((depths, 2, 2, 2, rows, width), jnp.bfloat16),
            pltpu.VMEM((depths, nf, piece, half), jnp.bfloat16),
            pltpu.VMEM((depths, nf - 1, piece, half), jnp.bfloat16),
            pltpu.VMEM((noff, -(-2 * per // 8) * 8, half), jnp.float32),
            pltpu.VMEM((depths, nf, image_piece, half), jnp.float32),
            pltpu.VMEM((depths, nf + 2 * edge, image_piece, half), jnp.float32),
            pltpu.VMEM((kper, rows + ofilt - 1, wide), jnp.float32),
            dma((depths * 4,)),
            dma((depths * 4,)),
            dma((depths * (nf - 1),)),
            dma((depths * (nf - 1),)),
            dma((depths * (nf - 1),)),
            dma((depths * (nf + 2 * edge),)),
            dma((depths * 2 * nf,)),
        ],
        compiler_params=pltpu.CompilerParams(
            collective_id=0, has_side_effects=True, vmem_limit_bytes=48 * 1024 * 1024
        ),
    )(source, receiver, taps, table_index, lags, offset_filters.transpose(1, 0, 2))


def solution(mesh):
    in_specs = (
        P("freq", None, "row", None),
        P("freq", None, "row", None),
        P("freq", None, None, None, None),
        P(None, "row", None),
        P(),
        P("freq", None, None),
    )
    out_specs = P(None, "freq", "row", None)
    return jax.shard_map(
        functools.partial(body, mesh.shape["freq"], mesh.shape["row"]),
        mesh=mesh,
        in_specs=in_specs,
        out_specs=out_specs,
        check_vma=False,
    )
```
